32 devices in a mesh: tile: 8 (over z, y), chan: 4 (over x, core).
Axes of the slice: x: 2, y: 2, z: 4, core: 2. Of those that a mesh axis runs over, the one named last changes fastest.
Arguments:
- seq_grad: bfloat16 [9216, 1536], P('tile', 'chan'), may hold values from -6 to 6
- token_slot: int32 [4608], P('tile'), may hold values from 0 to 9215, as said below
- pixels: bfloat16 [4608, 1536], P('tile', 'chan'), may hold values from -6 to 6
- dw_kernel: float32 [49, 1536], P(None, 'chan'), may hold values from -0.875 to 0.875
- ln_gain: float32 [1536], P('chan'), may hold values from 0.5 to 2
- ln_bias: float32 [1536], P('chan'), may hold values from -3 to 3
- w_in: bfloat16 [1536, 6144], P(None, 'chan'), may hold values from -0.15625 to 0.15625
- b_in: float32 [6144], P('chan'), may hold values from -3 to 3
- w_out: bfloat16 [6144, 1536], P('chan'), may hold values from -0.078125 to 0.078125
- layer_scale: float32 [1536], replicated, may hold values from 0.3 to 1.5
Outputs:
- grad_input: bfloat16 [4608, 1536], P('tile', 'chan')
- grad_w_in: float32 [1536, 6144], P('tile', 'chan')
- grad_w_out: float32 [6144, 1536], P('chan', 'tile')
- grad_kernel: float32 [49, 1536], P(None, 'chan')
The draws below stay inside these ranges and needn't reach their ends.
Inputs may be any that keep to these rules, and one draw needn't show every extreme that they name: No two visual tokens name the same slot. Slot s belongs to sequence shard s // 1152. The 576 tokens of one device (an aligned block of token_slot) take at most 144 slots of any one shard, and exactly 144 from some shard in every block.
All inputs are finite; a program needn't handle non-finite values.
Results may differ from the reference program's by a relative error of at most 0.015.
Values may be sent and summed in bfloat16 or wider, within the bound.
A program may use at most 128 MiB of HBM per device.

```python
import math
import jax
import jax.numpy as jnp
from jax import lax

C = 1536
HID = 6144
KSIZE = 7
PAGE_SIDE = 48
TOK_DEV = 576
TOKENS = 4608
PAGES = 2
CAP = 144
SLOTS = 1152
N_TILE = 8


def draw_token_slot(key, part):
    key = jax.random.fold_in(key, 11)
    seats = N_TILE * CAP
    hot_key, seat_key, order_key, slot_key = jax.random.split(key, 4)
    base = jax.random.randint(hot_key, (), 0, N_TILE)
    offsets = jax.random.randint(jax.random.fold_in(hot_key, 1), (N_TILE,), 0, max(1, N_TILE // 4))
    hot_source = (base + offsets) % N_TILE
    seat_ids = jnp.arange(seats, dtype=jnp.int32)

    def pick(tile_key, hot_one):
        scores = jax.random.permutation(tile_key, seats).astype(jnp.int32)
        scores = jnp.where(seat_ids // CAP == hot_one, scores - seats, scores)
        return jnp.argsort(scores, stable=True)[:TOK_DEV].astype(jnp.int32)
    chosen = jax.vmap(pick)(jax.random.split(seat_key, N_TILE), hot_source)
    shuffle = jax.vmap(lambda one_key: jax.random.permutation(one_key, TOK_DEV))(jax.random.split(order_key, N_TILE))
    chosen = jnp.take_along_axis(chosen, shuffle.astype(jnp.int32), axis=1)
    source = chosen // CAP
    ranks = chosen % CAP
    slot_perm = jax.vmap(lambda one_key: jax.random.permutation(one_key, SLOTS))(jax.random.split(slot_key, N_TILE)).astype(jnp.int32)
    tile_ids = jnp.arange(N_TILE, dtype=jnp.int32)[:, None]
    local_slot = slot_perm[source, tile_ids * CAP + ranks]
    return (source * SLOTS + local_slot).reshape(-1).astype(jnp.int32)


def block_scale(stream_key, shape, pieces, low, largest):
    def one(dim, shards_of):
        steps = jax.random.uniform(jax.random.fold_in(jax.random.fold_in(stream_key, 6), dim), (shards_of,), jnp.float32, low / len(pieces), largest / len(pieces))
        return jnp.repeat(jnp.exp(steps), shape[dim] // shards_of).reshape((-1,) + (1,) * (len(shape) - dim - 1))

    loudness = one(*pieces[0])
    for cut in pieces[1:]:
        loudness = loudness * one(*cut)
    return loudness


def centred(rng, extent, deviation, limit, cuts=(), kind=jnp.bfloat16):
    factor_of = block_scale(rng, extent, cuts, -0.22, 0.18) if cuts else 1.0
    values = jax.random.normal(rng, extent, jnp.float32) * deviation * factor_of
    return jnp.minimum(jnp.maximum(values, -limit), limit).astype(kind)


def setup_inputs(seed: int = 0) -> dict:
    streams_of = jax.random.split(jax.random.key(seed), 11)
    return {
        "seq_grad": centred(streams_of[0], (N_TILE * SLOTS, C), 1.0, 6.0, ((0, 8), (1, 4))),
        "token_slot": draw_token_slot(jax.random.fold_in(streams_of[10], 71), 0),
        "pixels": centred(streams_of[2], (TOKENS, C), 1.0, 6.0, ((0, 8), (1, 4))),
        "dw_kernel": centred(streams_of[3], (KSIZE * KSIZE, C), (KSIZE * KSIZE) ** -0.5, 0.875, ((1, 4),), jnp.float32),
        "ln_gain": jnp.clip(jnp.exp(math.log(2.0) - 1.3862944 * jax.random.uniform(streams_of[4], (C,), jnp.float32) ** block_scale(streams_of[4], (C,), ((0, 4),), -0.2, 0.2)), 0.5, 2.0),
        "ln_bias": centred(streams_of[5], (C,), 0.5, 3.0, ((0, 4),), jnp.float32),
        "w_in": centred(streams_of[6], (C, HID), C ** -0.5, 0.15625, ((1, 4),)),
        "b_in": centred(streams_of[7], (HID,), 0.5, 3.0, ((0, 4),), jnp.float32),
        "w_out": centred(streams_of[8], (HID, C), HID ** -0.5, 0.078125, ((0, 4),)),
        "layer_scale": jnp.clip(jnp.exp(jax.random.uniform(streams_of[9], (C,), jnp.float32, math.log(0.3), math.log(1.5))), 0.3, 1.5),
    }


EPS = 1e-06

def gelu_parts(preact):
    normal_cdf = 0.5 * (1.0 + jax.scipy.special.erf(preact * 0.7071067811865476))
    density = jnp.exp(-0.5 * preact * preact) * 0.3989422804014327
    return (preact * normal_cdf, normal_cdf + preact * density)

def depthwise(padded, kernel, side):
    total = jnp.zeros((padded.shape[0], side, side, padded.shape[3]), jnp.float32)
    for row_off in range(KSIZE):
        for col_off in range(KSIZE):
            window = padded[:, row_off:row_off + side, col_off:col_off + side, :]
            total = total + kernel[row_off * KSIZE + col_off] * window
    return total

def reference(seq_grad, token_slot, pixels, dw_kernel, ln_gain, ln_bias, w_in, b_in, w_out, layer_scale):
    side = PAGE_SIDE
    reach = KSIZE // 2
    upstream = jnp.take(seq_grad, token_slot, axis=0)
    canon = jnp.roll(pixels.astype(jnp.float32), TOK_DEV, axis=0)
    grid = canon.reshape(PAGES, side, side, C)
    padded = jnp.pad(grid, ((0, 0), (reach, reach), (reach, reach), (0, 0)))
    mixed = depthwise(padded, dw_kernel, side).reshape(TOKENS, C)
    center = mixed - lax.optimization_barrier(jnp.mean(mixed, axis=1, keepdims=True))
    inv_std = lax.rsqrt(lax.optimization_barrier(jnp.mean(center * center, axis=1, keepdims=True)) + EPS)
    normed = center * inv_std
    ln_out = (normed * ln_gain + ln_bias).astype(jnp.bfloat16)
    scaled = (upstream.astype(jnp.float32) * layer_scale).astype(jnp.bfloat16)
    scaled = jnp.roll(scaled, TOK_DEV, axis=0)

    def step(carry, inputs):
        acc_in, acc_out = carry
        rows_in, rows_up = inputs
        preact = jnp.dot(rows_in, w_in, preferred_element_type=jnp.float32) + b_in
        act_val, act_slope = gelu_parts(preact)
        hidden = act_val.astype(jnp.bfloat16)
        acc_out = acc_out + jnp.dot(hidden.T, rows_up, preferred_element_type=jnp.float32)
        back_hidden = jnp.dot(rows_up, w_out.T, preferred_element_type=jnp.float32)
        back_pre = (back_hidden * act_slope).astype(jnp.bfloat16)
        acc_in = acc_in + jnp.dot(rows_in.T, back_pre, preferred_element_type=jnp.float32)
        back_norm = jnp.dot(back_pre, w_in.T, preferred_element_type=jnp.float32)
        return ((acc_in, acc_out), back_norm)
    start = (jnp.zeros((C, HID), jnp.float32), jnp.zeros((HID, C), jnp.float32))
    blocks = (ln_out.reshape(PAGES, side * side, C), scaled.reshape(PAGES, side * side, C))
    (acc_in, acc_out), back_norm = lax.scan(step, start, blocks)
    back_norm = back_norm.reshape(TOKENS, C)
    grad_normed = back_norm * ln_gain
    mean_grad = lax.optimization_barrier(jnp.mean(grad_normed, axis=1, keepdims=True))
    mean_cross = lax.optimization_barrier(jnp.mean(grad_normed * normed, axis=1, keepdims=True))
    grad_mixed = inv_std * (grad_normed - mean_grad - normed * mean_cross)
    grad_grid = grad_mixed.reshape(PAGES, side, side, C)
    grad_pad = jnp.pad(grad_grid, ((0, 0), (reach, reach), (reach, reach), (0, 0)))
    back_conv = depthwise(grad_pad, dw_kernel[::-1], side).reshape(TOKENS, C)
    back_conv = jnp.roll(back_conv, -TOK_DEV, axis=0)
    grad_input = (upstream.astype(jnp.float32) + back_conv).astype(jnp.bfloat16)
    taps = []
    for row_off in range(KSIZE):
        for col_off in range(KSIZE):
            window = padded[:, row_off:row_off + side, col_off:col_off + side, :]
            taps.append(lax.optimization_barrier(jnp.sum(window * grad_grid, axis=(0, 1, 2))))
    factor = 1.0 / math.sqrt(TOKENS)
    grad_kernel = jnp.stack(taps) * factor
    return (grad_input, acc_in * factor, acc_out * factor, grad_kernel)
```

```python
import math

import jax
import jax.numpy as jnp
from jax import lax
from jax.sharding import PartitionSpec as P

C = 1536
KSIZE = 7
PAGE_SIDE = 48


EPS = 1e-06


def extended_2(value, sides, width):
    for axis, dim in sides:
        peers, length = (lax.axis_size(axis), value.shape[dim])
        up = [(i, (i + 1) % peers) for i in range(peers)]
        down = [(j, i) for i, j in up]
        last = lax.slice_in_dim(value, length - width, length, axis=dim)
        first = lax.slice_in_dim(value, 0, width, axis=dim)
        before = lax.ppermute(last, axis, up)
        after = lax.ppermute(first, axis, down)
        value = jnp.concatenate([before, value, after], axis=dim)
    return value


def gelu_parts(preact):
    normal_cdf = 0.5 * (1.0 + jax.scipy.special.erf(preact * 0.7071067811865476))
    density = jnp.exp(-0.5 * preact * preact) * 0.3989422804014327
    return (preact * normal_cdf, normal_cdf + preact * density)


def depthwise(padded, kernel, rows, cols):
    total = jnp.zeros((rows, cols, padded.shape[2]), jnp.float32)
    for row_off in range(KSIZE):
        for col_off in range(KSIZE):
            window = padded[row_off : row_off + rows, col_off : col_off + cols, :]
            total = total + kernel[row_off * KSIZE + col_off] * window
    return total


def page_edges(extended, band_index, tiles_page, reach):
    height = extended.shape[0]
    row_ids = lax.broadcasted_iota(jnp.int32, (height, 1, 1), 0)
    first = band_index % tiles_page == 0
    final = band_index % tiles_page == tiles_page - 1
    dropped = (row_ids < reach) & first | (row_ids >= height - reach) & final
    kept = jnp.where(dropped, jnp.zeros_like(extended), extended)
    return jnp.pad(kept, ((0, 0), (reach, reach), (0, 0)))


def pair_products(columns, values, factor):
    tiles = lax.axis_size("tile")
    tokens, width = columns.shape
    lines, rows = tiles // 2, width // tiles
    side = lax.axis_index("tile") % 2
    blocks = columns.reshape(tokens, lines, 2, rows)

    def product(which):
        part = lax.dynamic_index_in_dim(blocks, which, 2, keepdims=False)
        return (
            lax.dot_general(
                part.reshape(tokens, lines * rows),
                values,
                (((0,), (0,)), ((), ())),
                preferred_element_type=jnp.float32,
            )
            * factor
        )

    swap = [(i, i ^ 1) for i in range(tiles)]
    arrived = lax.ppermute(product(1 - side).astype(jnp.bfloat16), "tile", swap)
    total = product(side) + arrived.astype(jnp.float32)
    return total.reshape(lines, rows, values.shape[1])


def line_sum(parts):
    lines = parts.shape[0]
    tiles = lax.axis_size("tile")
    place = lax.axis_index("tile") // 2
    result = lax.dynamic_index_in_dim(parts, place, 0, keepdims=False)
    ups = downs = None
    for step in range(lines - 1):
        up_pairs = [(i, i + 2) for i in range(2 * (step + 1))]
        down_pairs = [(tiles - 1 - i, tiles - 1 - j) for i, j in up_pairs]
        far = jnp.clip(lines - 1 - step + place, 0, lines - 1)
        near = jnp.clip(step - (lines - 1 - place), 0, lines - 1)
        up = lax.dynamic_index_in_dim(parts, far, 0, keepdims=False)
        down = lax.dynamic_index_in_dim(parts, near, 0, keepdims=False)
        if step:
            up = up + ups.astype(jnp.float32)
            down = down + downs.astype(jnp.float32)
        ups = lax.ppermute(up.astype(jnp.bfloat16), "tile", up_pairs)
        downs = lax.ppermute(down.astype(jnp.bfloat16), "tile", down_pairs)
    return result + ups.astype(jnp.float32) + downs.astype(jnp.float32)


def shards(
    seq_grad, token_slot, pixels, dw_kernel, ln_gain, ln_bias, w_in, b_in, w_out, layer_scale
):
    tiles = lax.axis_size("tile")
    position = lax.axis_index("tile")
    band_index = (position + 1) % tiles
    slots = seq_grad.shape[0]
    capacity = slots // tiles
    tok_dev, chan_dev = pixels.shape
    reach = KSIZE // 2
    source = token_slot // slots
    local_slot = token_slot % slots
    onehot = (source[:, None] == jnp.arange(tiles, dtype=jnp.int32)[None, :]).astype(jnp.int32)
    ranks = jnp.sum((jnp.cumsum(onehot, axis=0) - onehot) * onehot, axis=1)
    seat = source * capacity + ranks
    request = (
        jnp.zeros((tiles * capacity,), jnp.int32).at[seat].set(local_slot).reshape(tiles, capacity)
    )
    found = jnp.take(
        seq_grad, lax.all_to_all(request, "tile", split_axis=0, concat_axis=0, tiled=True), axis=0
    )
    arrived = lax.all_to_all(found, "tile", split_axis=0, concat_axis=0, tiled=True)
    upstream = jnp.take(arrived.reshape(tiles * capacity, chan_dev), seat, axis=0)
    rows = tok_dev // PAGE_SIDE
    tiles_page = PAGE_SIDE // rows
    grid = pixels.reshape(rows, PAGE_SIDE, chan_dev)
    extended = extended_2(grid, (("tile", 0),), reach)
    padded = page_edges(extended.astype(jnp.float32), band_index, tiles_page, reach)
    mixed = depthwise(padded, dw_kernel, rows, PAGE_SIDE).reshape(tok_dev, chan_dev)
    own_mean = jnp.mean(mixed, axis=1)
    own_center = mixed - own_mean[:, None]
    own_spread = jnp.sum(own_center * own_center, axis=1)
    stats = lax.all_gather(jnp.stack([own_mean, own_spread]), "chan")
    mean = jnp.mean(stats[:, 0], axis=0)
    shift = stats[:, 0] - mean
    spread = jnp.sum(stats[:, 1] + chan_dev * shift * shift, axis=0)
    center = mixed - mean[:, None]
    inv_std = lax.rsqrt(spread / C + EPS)[:, None]
    normed = center * inv_std
    ln_part = (normed * ln_gain + ln_bias).astype(jnp.bfloat16)
    ln_out, upstream_all = (
        lax.all_gather(ln_part, "chan", axis=1, tiled=True),
        lax.all_gather(upstream, "chan", axis=1, tiled=True),
    )
    scaled = (upstream_all.astype(jnp.float32) * layer_scale).astype(jnp.bfloat16)
    preact = jnp.dot(ln_out, w_in, preferred_element_type=jnp.float32) + b_in
    act_val, act_slope = gelu_parts(preact)
    hidden = act_val.astype(jnp.bfloat16)
    factor = 1.0 / math.sqrt(tok_dev * tiles)
    out_parts = pair_products(scaled, hidden, factor)
    back_hidden = lax.dot_general(
        scaled, w_out, (((1,), (1,)), ((), ())), preferred_element_type=jnp.float32
    )
    back_pre = (back_hidden * act_slope).astype(jnp.bfloat16)
    partial_sum = lax.dot_general(
        back_pre, w_in, (((1,), (1,)), ((), ())), preferred_element_type=jnp.float32
    )
    back_norm = lax.psum_scatter(
        partial_sum.astype(jnp.bfloat16), "chan", scatter_dimension=1, tiled=True
    ).astype(jnp.float32)
    in_parts = pair_products(ln_out, back_pre, factor)
    grad_w_out = line_sum(out_parts).T
    grad_w_in = line_sum(in_parts)
    grad_normed = back_norm * ln_gain
    sum_grad, sum_cross = lax.psum(
        (jnp.sum(grad_normed, axis=1), jnp.sum(grad_normed * normed, axis=1)), "chan"
    )
    grad_mixed = inv_std * (
        grad_normed - (sum_grad / C)[:, None] - normed * (sum_cross / C)[:, None]
    )
    grad_grid = grad_mixed.reshape(rows, PAGE_SIDE, chan_dev)
    grad_ext = extended_2(grad_grid.astype(jnp.bfloat16), (("tile", 0),), reach).astype(
        grad_grid.dtype
    )
    grad_pad = page_edges(grad_ext, band_index, tiles_page, reach)
    back_conv = depthwise(grad_pad, dw_kernel[::-1], rows, PAGE_SIDE).reshape(tok_dev, chan_dev)
    grad_input = (upstream.astype(jnp.float32) + back_conv).astype(jnp.bfloat16)
    taps = []
    for row_off in range(KSIZE):
        for col_off in range(KSIZE):
            window = padded[row_off : row_off + rows, col_off : col_off + PAGE_SIDE, :]
            taps.append(jnp.sum(window * grad_grid, axis=(0, 1)))
    grad_kernel = lax.psum(jnp.stack(taps) * factor, "tile")
    return (grad_input, grad_w_in, grad_w_out, grad_kernel)


def solution(mesh):
    placed = (
        P("tile", "chan"),
        P("tile"),
        P("tile", "chan"),
        P(None, "chan"),
        P("chan"),
        P("chan"),
        P(None, "chan"),
        P("chan"),
        P("chan", None),
        P(),
    )
    return jax.shard_map(
        shards,
        mesh=mesh,
        in_specs=placed,
        out_specs=(P("tile", "chan"), P("tile", "chan"), P("chan", "tile"), P(None, "chan")),
        check_vma=False,
    )
```

```python
import math

import jax
import jax.numpy as jnp
from jax import lax
from jax.sharding import PartitionSpec as P

C = 1536
KSIZE = 7
PAGE_SIDE = 48


EPS = 1e-06


def extended_2(value, sides, width):
    for axis, dim in sides:
        peers, length = (lax.axis_size(axis), value.shape[dim])
        up = [(i, (i + 1) % peers) for i in range(peers)]
        down = [(j, i) for i, j in up]
        last = lax.slice_in_dim(value, length - width, length, axis=dim)
        first = lax.slice_in_dim(value, 0, width, axis=dim)
        before = lax.ppermute(last, axis, up)
        after = lax.ppermute(first, axis, down)
        value = jnp.concatenate([before, value, after], axis=dim)
    return value


def gelu_parts(preact):
    normal_cdf = 0.5 * (1.0 + jax.scipy.special.erf(preact * 0.7071067811865476))
    density = jnp.exp(-0.5 * preact * preact) * 0.3989422804014327
    return (preact * normal_cdf, normal_cdf + preact * density)


def depthwise(padded, kernel, rows, cols):
    total = jnp.zeros((rows, cols, padded.shape[2]), jnp.float32)
    for row_off in range(KSIZE):
        for col_off in range(KSIZE):
            window = padded[row_off : row_off + rows, col_off : col_off + cols, :]
            total = total + kernel[row_off * KSIZE + col_off] * window
    return total


def page_edges(extended, band_index, tiles_page, reach):
    height = extended.shape[0]
    row_ids = lax.broadcasted_iota(jnp.int32, (height, 1, 1), 0)
    first = band_index % tiles_page == 0
    final = band_index % tiles_page == tiles_page - 1
    dropped = (row_ids < reach) & first | (row_ids >= height - reach) & final
    kept = jnp.where(dropped, jnp.zeros_like(extended), extended)
    return jnp.pad(kept, ((0, 0), (reach, reach), (0, 0)))


def after(value, *others):
    return lax.optimization_barrier((value, *others))[0]


def product(columns, values, factor):
    return (
        lax.dot_general(
            columns, values, (((0,), (0,)), ((), ())), preferred_element_type=jnp.float32
        )
        * factor
    )


def pair_swap(value):
    swap = [(i, i ^ 1) for i in range(lax.axis_size("tile"))]
    return lax.ppermute(value.astype(jnp.bfloat16), "tile", swap)


def pair_columns(columns):
    tiles = lax.axis_size("tile")
    tokens, width = columns.shape
    side = lax.axis_index("tile") % 2
    blocks = columns.reshape(tokens, tiles // 2, 2, width // tiles)
    return [
        lax.dynamic_index_in_dim(blocks, which, 2, keepdims=False).reshape(tokens, width // 2)
        for which in (side, 1 - side)
    ]


class LineSum:
    def __init__(self, parts):
        self.lines = lax.axis_size("tile") // 2
        self.parts = parts.reshape(self.lines, -1, parts.shape[-1])
        self.place = lax.axis_index("tile") // 2
        self.step = 0
        self.ups = self.downs = None

    def pick(self, index):
        return lax.dynamic_index_in_dim(self.parts, index, 0, keepdims=False)

    def advance(self, *others):
        lines, tiles, step = self.lines, 2 * self.lines, self.step
        up_pairs = [(i, i + 2) for i in range(2 * (step + 1))]
        down_pairs = [(tiles - 1 - i, tiles - 1 - j) for i, j in up_pairs]
        up = self.pick(jnp.clip(lines - 1 - step + self.place, 0, lines - 1))
        down = self.pick(jnp.clip(step - (lines - 1 - self.place), 0, lines - 1))
        if step:
            ups, downs = self.arrived(*others)
            up, down = up + ups, down + downs
        up, down = lax.optimization_barrier((up.astype(jnp.bfloat16), down.astype(jnp.bfloat16)))
        self.ups = lax.ppermute(up, "tile", up_pairs)
        self.downs = lax.ppermute(down, "tile", down_pairs)
        self.step += 1
        return up

    def arrived(self, *others):
        ups, downs = self.ups, self.downs
        if others:
            ups, downs = lax.optimization_barrier((ups, downs, *others))[:2]
        return ups.astype(jnp.float32), downs.astype(jnp.float32)

    def finish(self, *others):
        while self.step < self.lines - 1:
            self.advance(*others)
        ups, downs = self.arrived(*others)
        return self.pick(self.place) + ups + downs


def shards(
    seq_grad, token_slot, pixels, dw_kernel, ln_gain, ln_bias, w_in, b_in, w_out, layer_scale
):
    tiles = lax.axis_size("tile")
    position = lax.axis_index("tile")
    band_index = (position + 1) % tiles
    slots = seq_grad.shape[0]
    capacity = slots // tiles
    tok_dev, chan_dev = pixels.shape
    reach = KSIZE // 2
    source = token_slot // slots
    local_slot = token_slot % slots
    onehot = (source[:, None] == jnp.arange(tiles, dtype=jnp.int32)[None, :]).astype(jnp.int32)
    ranks = jnp.sum((jnp.cumsum(onehot, axis=0) - onehot) * onehot, axis=1)
    seat = source * capacity + ranks
    seats = jnp.arange(tiles * capacity, dtype=jnp.int32)
    placed = seat[:, None] == seats[None, :]
    request = jnp.sum(jnp.where(placed, local_slot[:, None], 0), axis=0).reshape(tiles, capacity)
    asked = lax.all_to_all(request, "tile", split_axis=0, concat_axis=0, tiled=True)
    wanted = asked.reshape(-1, 1) == jnp.arange(slots, dtype=jnp.int32)[None, :]
    found = jnp.dot(
        wanted.astype(jnp.bfloat16), seq_grad, preferred_element_type=jnp.float32
    ).astype(jnp.bfloat16)
    arrived = lax.all_to_all(
        found.reshape(tiles, capacity, chan_dev), "tile", split_axis=0, concat_axis=0, tiled=True
    )
    rows = tok_dev // PAGE_SIDE
    tiles_page = PAGE_SIDE // rows
    grid = pixels.reshape(rows, PAGE_SIDE, chan_dev)
    extended = extended_2(grid, (("tile", 0),), reach)
    extended = after(extended, found)
    padded = page_edges(extended.astype(jnp.float32), band_index, tiles_page, reach)
    mixed = depthwise(padded, dw_kernel, rows, PAGE_SIDE).reshape(tok_dev, chan_dev)
    own_mean = jnp.mean(mixed, axis=1)
    own_center = mixed - own_mean[:, None]
    own_spread = jnp.sum(own_center * own_center, axis=1)
    stats = lax.all_gather(jnp.stack([own_mean, own_spread]), "chan")
    mean = jnp.mean(stats[:, 0], axis=0)
    shift = stats[:, 0] - mean
    spread = jnp.sum(stats[:, 1] + chan_dev * shift * shift, axis=0)
    center = mixed - mean[:, None]
    inv_std = lax.rsqrt(spread / C + EPS)[:, None]
    normed = center * inv_std
    ln_part = (normed * ln_gain + ln_bias).astype(jnp.bfloat16)
    ln_out = lax.all_gather(ln_part, "chan", axis=1, tiled=True)
    arrived = after(arrived, ln_part)
    upstream = jnp.dot(
        placed.astype(jnp.bfloat16),
        arrived.reshape(tiles * capacity, chan_dev),
        preferred_element_type=jnp.float32,
    ).astype(jnp.bfloat16)
    upstream_all = lax.all_gather(upstream, "chan", axis=1, tiled=True)
    scaled = (upstream_all.astype(jnp.float32) * layer_scale).astype(jnp.bfloat16)
    preact = jnp.dot(ln_out, w_in, preferred_element_type=jnp.float32) + b_in
    act_val, act_slope = gelu_parts(preact)
    hidden = act_val.astype(jnp.bfloat16)
    factor = 1.0 / math.sqrt(tok_dev * tiles)
    scaled_own, scaled_other = pair_columns(scaled)
    out_send, hidden = lax.optimization_barrier(
        (product(scaled_other, hidden, factor).astype(jnp.bfloat16), hidden)
    )
    out_swap = pair_swap(out_send)
    back_hidden = lax.dot_general(
        after(scaled, out_send), w_out, (((1,), (1,)), ((), ())), preferred_element_type=jnp.float32
    )
    back_pre = (back_hidden * act_slope).astype(jnp.bfloat16)
    half = back_pre.shape[1] // 2
    lead = LineSum(product(ln_out, back_pre[:, :half], factor))
    sent = lead.advance()
    back_pre_late = after(back_pre, sent)
    partial_sum = lax.dot_general(
        back_pre_late, w_in, (((1,), (1,)), ((), ())), preferred_element_type=jnp.float32
    )
    partial_sum = partial_sum.astype(jnp.bfloat16)
    back_norm = lax.psum_scatter(partial_sum, "chan", scatter_dimension=1, tiled=True)
    ln_own, ln_other = pair_columns(ln_out)
    in_send = after(product(ln_other, back_pre[:, half:], factor).astype(jnp.bfloat16), partial_sum)
    in_swap = pair_swap(in_send)
    out_part = product(scaled_own, hidden, factor)
    in_part = product(ln_own, back_pre[:, half:], factor)
    sent = lead.advance(in_send)
    while lead.step < lead.lines - 1:
        sent = lead.advance(sent)
    back_norm = after(back_norm, sent).astype(jnp.float32)
    grad_normed = back_norm * ln_gain
    sum_grad, sum_cross = lax.psum(
        (jnp.sum(grad_normed, axis=1), jnp.sum(grad_normed * normed, axis=1)), "chan"
    )
    grad_mixed = inv_std * (
        grad_normed - (sum_grad / C)[:, None] - normed * (sum_cross / C)[:, None]
    )
    grad_grid = grad_mixed.reshape(rows, PAGE_SIDE, chan_dev)
    taps = []
    for row_off in range(KSIZE):
        for col_off in range(KSIZE):
            window = padded[row_off : row_off + rows, col_off : col_off + PAGE_SIDE, :]
            taps.append(jnp.sum(window * grad_grid, axis=(0, 1)))
    taps = jnp.stack(taps) * factor
    grad_kernel = lax.psum(taps, "tile")
    grad_ext = extended_2(grad_grid.astype(jnp.bfloat16), (("tile", 0),), reach)
    out_line = LineSum(out_part + after(out_swap, taps).astype(jnp.float32))
    sent = out_line.advance()
    lead_sum = lead.finish(sent).reshape(2, -1, half)
    side = lax.axis_index("tile") % 2
    lead_other = lax.dynamic_index_in_dim(lead_sum, 1 - side, 0, keepdims=False)
    lead_own = lax.dynamic_index_in_dim(lead_sum, side, 0, keepdims=False)
    lead_swap = pair_swap(lead_other)
    grad_pad = page_edges(
        after(grad_ext, sent).astype(jnp.float32), band_index, tiles_page, reach
    )
    back_conv = depthwise(grad_pad, dw_kernel[::-1], rows, PAGE_SIDE).reshape(tok_dev, chan_dev)
    grad_input = (upstream.astype(jnp.float32) + back_conv).astype(jnp.bfloat16)
    sent = out_line.advance(grad_input)
    in_line = LineSum(in_part + after(in_swap, sent).astype(jnp.float32))
    in_line.advance()
    out_line.advance()
    in_line.advance()
    grad_w_out = out_line.finish().T
    in_late = in_line.finish()
    in_early = lead_own + lead_swap.astype(jnp.float32)
    grad_w_in = jnp.concatenate([in_early, in_late], axis=1)
    return (grad_input, grad_w_in, grad_w_out, grad_kernel)


def solution(mesh):
    placed = (
        P("tile", "chan"),
        P("tile"),
        P("tile", "chan"),
        P(None, "chan"),
        P("chan"),
        P("chan"),
        P(None, "chan"),
        P("chan"),
        P("chan", None),
        P(),
    )
    return jax.shard_map(
        shards,
        mesh=mesh,
        in_specs=placed,
        out_specs=(P("tile", "chan"), P("tile", "chan"), P("chan", "tile"), P(None, "chan")),
        check_vma=False,
    )
```

```python
import functools
import math

import jax
import jax.numpy as jnp
from jax import lax
from jax.experimental import pallas as pl
from jax.experimental.pallas import tpu as pltpu
from jax.sharding import PartitionSpec as P

C = 1536
KSIZE = 7
PAGE_SIDE = 48


EPS = 1e-06


def extended_2(value, sides, width):
    for axis, dim in sides:
        peers, length = (lax.axis_size(axis), value.shape[dim])
        up = [(i, (i + 1) % peers) for i in range(peers)]
        down = [(j, i) for i, j in up]
        last = lax.slice_in_dim(value, length - width, length, axis=dim)
        first = lax.slice_in_dim(value, 0, width, axis=dim)
        before = lax.ppermute(last, axis, up)
        after = lax.ppermute(first, axis, down)
        value = jnp.concatenate([before, value, after], axis=dim)
    return value


def gelu_parts(preact):
    normal_cdf = 0.5 * (1.0 + jax.scipy.special.erf(preact * 0.7071067811865476))
    density = jnp.exp(-0.5 * preact * preact) * 0.3989422804014327
    return (preact * normal_cdf, normal_cdf + preact * density)


def depthwise(padded, kernel, rows, cols):
    total = jnp.zeros((rows, cols, padded.shape[2]), jnp.float32)
    for row_off in range(KSIZE):
        for col_off in range(KSIZE):
            window = padded[row_off : row_off + rows, col_off : col_off + cols, :]
            total = total + kernel[row_off * KSIZE + col_off] * window
    return total


def page_edges(extended, band_index, tiles_page, reach):
    height = extended.shape[0]
    row_ids = lax.broadcasted_iota(jnp.int32, (height, 1, 1), 0)
    first = band_index % tiles_page == 0
    final = band_index % tiles_page == tiles_page - 1
    dropped = (row_ids < reach) & first | (row_ids >= height - reach) & final
    kept = jnp.where(dropped, jnp.zeros_like(extended), extended)
    return jnp.pad(kept, ((0, 0), (reach, reach), (0, 0)))


def after(value, *others):
    return lax.optimization_barrier((value, *others))[0]


LINES = 4
CHUNK = 256
MESH = pl.DeviceIdType.MESH


def sum_kernel(
    factor, columns, values, out, pair_out, pair_in, parts, up_out, up_in, down_out, down_in,
    pair_sent, pair_got, up_sent, up_got, down_sent, down_got,
):
    me = lax.axis_index("tile")
    side, place = me % 2, me // 2
    rows = columns.shape[0] // (2 * LINES)
    chunks = values.shape[1] // CHUNK
    pair = me + 1 - 2 * side
    has_up, has_down = place < LINES - 1, place > 0

    barrier = pltpu.get_barrier_semaphore()
    pl.semaphore_signal(barrier, inc=1, device_id={"tile": pair}, device_id_type=MESH)

    @pl.when(has_up)
    def _():
        pl.semaphore_signal(barrier, inc=1, device_id={"tile": me + 2}, device_id_type=MESH)

    @pl.when(has_down)
    def _():
        pl.semaphore_signal(barrier, inc=1, device_id={"tile": me - 2}, device_id_type=MESH)

    @pl.when(has_up & has_down)
    def _():
        pl.semaphore_wait(barrier, 3)

    @pl.when(jnp.logical_not(has_up & has_down))
    def _():
        pl.semaphore_wait(barrier, 2)

    def swap(j):
        return pltpu.make_async_remote_copy(
            src_ref=pair_out.at[j],
            dst_ref=pair_in.at[j],
            send_sem=pair_sent.at[j],
            recv_sem=pair_got.at[j],
            device_id={"tile": pair},
            device_id_type=MESH,
        )

    def hop(upward, j, step):
        src, dst, sent, got, peer = (
            (up_out, up_in, up_sent, up_got, me + 2)
            if upward
            else (down_out, down_in, down_sent, down_got, me - 2)
        )
        return pltpu.make_async_remote_copy(
            src_ref=src.at[j, step],
            dst_ref=dst.at[j, step],
            send_sem=sent.at[j, step],
            recv_sem=got.at[j, step],
            device_id={"tile": peer},
            device_id_type=MESH,
        )

    def block(line, which, j):
        start = pl.multiple_of((2 * line + which) * rows, rows)
        return (
            jnp.dot(
                columns[pl.ds(start, rows), :],
                values[:, j * CHUNK : (j + 1) * CHUNK],
                preferred_element_type=jnp.float32,
            )
            * factor
        )

    for j in range(chunks):
        for line in range(LINES):
            pair_out[j, line] = block(line, 1 - side, j).astype(jnp.bfloat16)
        swap(j).start()
    for j in range(chunks):
        for line in range(LINES):
            parts[j, line] = block(line, side, j)

    def take(j):
        swap(j).wait_recv()
        parts[j] = parts[j] + pair_in[j].astype(jnp.float32)

    def send(j, step):
        for upward in (True, False):
            back = place if upward else LINES - 1 - place

            @pl.when(back <= step)
            def _(upward=upward, back=back):
                dest = LINES - 1 - step + place if upward else step - back
                total = up_out if upward else down_out
                total[j, step] = parts[j, dest].astype(jnp.bfloat16)

                if step:

                    @pl.when(back > 0)
                    def _():
                        hop(upward, j, step - 1).wait_recv()
                        got = up_in if upward else down_in
                        total[j, step] = (
                            parts[j, dest] + got[j, step - 1].astype(jnp.float32)
                        ).astype(jnp.bfloat16)

                hop(upward, j, step).start()

    def finish(j):
        where = pl.ds(j * CHUNK, CHUNK)
        out[:, where] = parts[j, place]

        @pl.when(has_down)
        def _():
            hop(True, j, LINES - 2).wait_recv()
            out[:, where] += up_in[j, LINES - 2].astype(jnp.float32)

        @pl.when(has_up)
        def _():
            hop(False, j, LINES - 2).wait_recv()
            out[:, where] += down_in[j, LINES - 2].astype(jnp.float32)

    for turn in range(chunks + 1):
        if turn < chunks:
            take(turn)
            send(turn, 0)
        if turn > 0:
            send(turn - 1, 2)
        if turn < chunks:
            send(turn, 1)
        if turn > 0:
            finish(turn - 1)
    for j in range(chunks):
        swap(j).wait_send()
        for step in range(LINES - 1):

            @pl.when(place <= step)
            def _(j=j, step=step):
                hop(True, j, step).wait_send()

            @pl.when(LINES - 1 - place <= step)
            def _(j=j, step=step):
                hop(False, j, step).wait_send()


def summed_product(columns, values, factor, ident):
    tiles = lax.axis_size("tile")
    (tokens, width), depth = columns.shape, values.shape[1]
    rows = width // tiles
    if tiles != 2 * LINES or rows % 16 or depth % CHUNK:
        whole = lax.dot_general(
            columns, values, (((0,), (0,)), ((), ())), preferred_element_type=jnp.float32
        )
        return lax.psum_scatter(whole * factor, "tile", scatter_dimension=0, tiled=True)
    chunks, hops = depth // CHUNK, LINES - 1
    line_buffer = pltpu.VMEM((chunks, hops, rows, CHUNK), jnp.bfloat16)
    pair_buffer = pltpu.VMEM((chunks, LINES, rows, CHUNK), jnp.bfloat16)
    return pl.pallas_call(
        functools.partial(sum_kernel, factor),
        out_shape=jax.ShapeDtypeStruct((rows, depth), jnp.float32),
        in_specs=[pl.BlockSpec(memory_space=pltpu.VMEM)] * 2,
        out_specs=pl.BlockSpec(memory_space=pltpu.VMEM),
        scratch_shapes=[
            pair_buffer,
            pair_buffer,
            pltpu.VMEM((chunks, LINES, rows, CHUNK), jnp.float32),
            *([line_buffer] * 4),
            *([pltpu.SemaphoreType.DMA((chunks,))] * 2),
            *([pltpu.SemaphoreType.DMA((chunks, hops))] * 4),
        ],
        compiler_params=pltpu.CompilerParams(
            collective_id=ident, has_side_effects=True, vmem_limit_bytes=36 * 1024 * 1024
        ),
        cost_estimate=pl.CostEstimate(
            flops=2 * tokens * width * depth,
            bytes_accessed=100_000_000,
            transcendentals=0,
        ),
    )(columns.T, values)


def shards(
    seq_grad, token_slot, pixels, dw_kernel, ln_gain, ln_bias, w_in, b_in, w_out, layer_scale
):
    tiles = lax.axis_size("tile")
    position = lax.axis_index("tile")
    band_index = (position + 1) % tiles
    slots = seq_grad.shape[0]
    capacity = slots // tiles
    tok_dev, chan_dev = pixels.shape
    reach = KSIZE // 2
    source = token_slot // slots
    local_slot = token_slot % slots
    onehot = (source[:, None] == jnp.arange(tiles, dtype=jnp.int32)[None, :]).astype(jnp.int32)
    ranks = jnp.sum((jnp.cumsum(onehot, axis=0) - onehot) * onehot, axis=1)
    seat = source * capacity + ranks
    seats = jnp.arange(tiles * capacity, dtype=jnp.int32)
    placed = seat[:, None] == seats[None, :]
    request = jnp.sum(jnp.where(placed, local_slot[:, None], 0), axis=0).reshape(tiles, capacity)
    asked = lax.all_to_all(request, "tile", split_axis=0, concat_axis=0, tiled=True)
    wanted = asked.reshape(-1, 1) == jnp.arange(slots, dtype=jnp.int32)[None, :]
    found = jnp.dot(
        wanted.astype(jnp.bfloat16), seq_grad, preferred_element_type=jnp.float32
    ).astype(jnp.bfloat16)
    arrived = lax.all_to_all(
        found.reshape(tiles, capacity, chan_dev), "tile", split_axis=0, concat_axis=0, tiled=True
    )
    rows = tok_dev // PAGE_SIDE
    tiles_page = PAGE_SIDE // rows
    grid = pixels.reshape(rows, PAGE_SIDE, chan_dev)
    extended = extended_2(grid, (("tile", 0),), reach)
    extended = after(extended, found)
    padded = page_edges(extended.astype(jnp.float32), band_index, tiles_page, reach)
    mixed = depthwise(padded, dw_kernel, rows, PAGE_SIDE).reshape(tok_dev, chan_dev)
    own_mean = jnp.mean(mixed, axis=1)
    own_center = mixed - own_mean[:, None]
    own_spread = jnp.sum(own_center * own_center, axis=1)
    stats = lax.all_gather(jnp.stack([own_mean, own_spread]), "chan")
    mean = jnp.mean(stats[:, 0], axis=0)
    shift = stats[:, 0] - mean
    spread = jnp.sum(stats[:, 1] + chan_dev * shift * shift, axis=0)
    center = mixed - mean[:, None]
    inv_std = lax.rsqrt(spread / C + EPS)[:, None]
    normed = center * inv_std
    ln_part = (normed * ln_gain + ln_bias).astype(jnp.bfloat16)
    ln_out = lax.all_gather(ln_part, "chan", axis=1, tiled=True)
    arrived = after(arrived, ln_part)
    upstream = jnp.dot(
        placed.astype(jnp.bfloat16),
        arrived.reshape(tiles * capacity, chan_dev),
        preferred_element_type=jnp.float32,
    ).astype(jnp.bfloat16)
    upstream_all = lax.all_gather(upstream, "chan", axis=1, tiled=True)
    scaled = (upstream_all.astype(jnp.float32) * layer_scale).astype(jnp.bfloat16)
    preact = jnp.dot(ln_out, w_in, preferred_element_type=jnp.float32) + b_in
    act_val, act_slope = gelu_parts(preact)
    hidden = act_val.astype(jnp.bfloat16)
    factor = 1.0 / math.sqrt(tok_dev * tiles)
    back_hidden = lax.dot_general(
        scaled, w_out, (((1,), (1,)), ((), ())), preferred_element_type=jnp.float32
    )
    back_pre = (back_hidden * act_slope).astype(jnp.bfloat16)
    partial_sum = lax.dot_general(
        back_pre, w_in, (((1,), (1,)), ((), ())), preferred_element_type=jnp.float32
    ).astype(jnp.bfloat16)
    back_norm = lax.psum_scatter(partial_sum, "chan", scatter_dimension=1, tiled=True)
    grad_w_out = summed_product(scaled, after(hidden, partial_sum), factor, 0)
    back_norm = after(back_norm, grad_w_out).astype(jnp.float32)
    grad_normed = back_norm * ln_gain
    sum_grad, sum_cross = lax.psum(
        (jnp.sum(grad_normed, axis=1), jnp.sum(grad_normed * normed, axis=1)), "chan"
    )
    grad_mixed = inv_std * (
        grad_normed - (sum_grad / C)[:, None] - normed * (sum_cross / C)[:, None]
    )
    grad_grid = grad_mixed.reshape(rows, PAGE_SIDE, chan_dev)
    taps = []
    for row_off in range(KSIZE):
        for col_off in range(KSIZE):
            window = padded[row_off : row_off + rows, col_off : col_off + PAGE_SIDE, :]
            taps.append(jnp.sum(window * grad_grid, axis=(0, 1)))
    taps = jnp.stack(taps) * factor
    grad_kernel = lax.psum(taps, "tile")
    grad_ext = extended_2(grad_grid.astype(jnp.bfloat16), (("tile", 0),), reach)
    grad_w_in = summed_product(ln_out, after(back_pre, taps, grad_mixed), factor, 1)
    grad_pad = page_edges(
        after(grad_ext, grad_w_in).astype(jnp.float32), band_index, tiles_page, reach
    )
    back_conv = depthwise(grad_pad, dw_kernel[::-1], rows, PAGE_SIDE).reshape(tok_dev, chan_dev)
    grad_input = (upstream.astype(jnp.float32) + back_conv).astype(jnp.bfloat16)
    return (grad_input, grad_w_in, grad_w_out.T, grad_kernel)


def solution(mesh):
    placed = (
        P("tile", "chan"),
        P("tile"),
        P("tile", "chan"),
        P(None, "chan"),
        P("chan"),
        P("chan"),
        P(None, "chan"),
        P("chan"),
        P("chan", None),
        P(),
    )
    return jax.shard_map(
        shards,
        mesh=mesh,
        in_specs=placed,
        out_specs=(P("tile", "chan"), P("tile", "chan"), P("chan", "tile"), P(None, "chan")),
        check_vma=False,
    )
```

```python
import functools
import math

import jax
import jax.numpy as jnp
from jax import lax
from jax.experimental import pallas as pl
from jax.experimental.pallas import tpu as pltpu
from jax.sharding import PartitionSpec as P

C = 1536
KSIZE = 7
PAGE_SIDE = 48


EPS = 1e-06


def extended_2(value, sides, width):
    for axis, dim in sides:
        peers, length = (lax.axis_size(axis), value.shape[dim])
        up = [(i, (i + 1) % peers) for i in range(peers)]
        down = [(j, i) for i, j in up]
        last = lax.slice_in_dim(value, length - width, length, axis=dim)
        first = lax.slice_in_dim(value, 0, width, axis=dim)
        before = lax.ppermute(last, axis, up)
        after = lax.ppermute(first, axis, down)
        value = jnp.concatenate([before, value, after], axis=dim)
    return value


def gelu_parts(preact):
    normal_cdf = 0.5 * (1.0 + jax.scipy.special.erf(preact * 0.7071067811865476))
    density = jnp.exp(-0.5 * preact * preact) * 0.3989422804014327
    return (preact * normal_cdf, normal_cdf + preact * density)


def depthwise(padded, kernel, rows, cols):
    total = jnp.zeros((rows, cols, padded.shape[2]), jnp.float32)
    for row_off in range(KSIZE):
        for col_off in range(KSIZE):
            window = padded[row_off : row_off + rows, col_off : col_off + cols, :]
            total = total + kernel[row_off * KSIZE + col_off] * window
    return total


def page_edges(extended, band_index, tiles_page, reach):
    height = extended.shape[0]
    row_ids = lax.broadcasted_iota(jnp.int32, (height, 1, 1), 0)
    first = band_index % tiles_page == 0
    final = band_index % tiles_page == tiles_page - 1
    dropped = (row_ids < reach) & first | (row_ids >= height - reach) & final
    kept = jnp.where(dropped, jnp.zeros_like(extended), extended)
    return jnp.pad(kept, ((0, 0), (reach, reach), (0, 0)))


def after(value, *others):
    return lax.optimization_barrier((value, *others))[0]


LINES = 4
CHUNK = 256
MESH = pl.DeviceIdType.MESH


def sum_kernel(
    factor, columns, values, out, pair_out, pair_in, parts, up_out, up_in, down_out, down_in,
    pair_sent, pair_got, up_sent, up_got, down_sent, down_got,
):
    me = lax.axis_index("tile")
    side, place = me % 2, me // 2
    rows = columns.shape[0] // (2 * LINES)
    chunks = values.shape[1] // CHUNK
    pair = me + 1 - 2 * side
    has_up, has_down = place < LINES - 1, place > 0

    barrier = pltpu.get_barrier_semaphore()
    pl.semaphore_signal(barrier, inc=1, device_id={"tile": pair}, device_id_type=MESH)

    @pl.when(has_up)
    def _():
        pl.semaphore_signal(barrier, inc=1, device_id={"tile": me + 2}, device_id_type=MESH)

    @pl.when(has_down)
    def _():
        pl.semaphore_signal(barrier, inc=1, device_id={"tile": me - 2}, device_id_type=MESH)

    @pl.when(has_up & has_down)
    def _():
        pl.semaphore_wait(barrier, 3)

    @pl.when(jnp.logical_not(has_up & has_down))
    def _():
        pl.semaphore_wait(barrier, 2)

    def swap(j):
        return pltpu.make_async_remote_copy(
            src_ref=pair_out.at[j],
            dst_ref=pair_in.at[j],
            send_sem=pair_sent.at[j],
            recv_sem=pair_got.at[j],
            device_id={"tile": pair},
            device_id_type=MESH,
        )

    def hop(upward, j, step):
        src, dst, sent, got, peer = (
            (up_out, up_in, up_sent, up_got, me + 2)
            if upward
            else (down_out, down_in, down_sent, down_got, me - 2)
        )
        return pltpu.make_async_remote_copy(
            src_ref=src.at[j, step],
            dst_ref=dst.at[j, step],
            send_sem=sent.at[j, step],
            recv_sem=got.at[j, step],
            device_id={"tile": peer},
            device_id_type=MESH,
        )

    def block(line, which, j):
        start = pl.multiple_of((2 * line + which) * rows, rows)
        return (
            jnp.dot(
                columns[pl.ds(start, rows), :],
                values[:, j * CHUNK : (j + 1) * CHUNK],
                preferred_element_type=jnp.float32,
            )
            * factor
        )

    for j in range(chunks):
        for line in range(LINES):
            pair_out[j, line] = block(line, 1 - side, j).astype(jnp.bfloat16)
        swap(j).start()
    for j in range(chunks):
        for line in range(LINES):
            parts[j, line] = block(line, side, j)

    def take(j):
        swap(j).wait_recv()
        parts[j] = parts[j] + pair_in[j].astype(jnp.float32)

    def send(j, step):
        for upward in (True, False):
            back = place if upward else LINES - 1 - place

            @pl.when(back <= step)
            def _(upward=upward, back=back):
                dest = LINES - 1 - step + place if upward else step - back
                total = up_out if upward else down_out
                total[j, step] = parts[j, dest].astype(jnp.bfloat16)

                if step:

                    @pl.when(back > 0)
                    def _():
                        hop(upward, j, step - 1).wait_recv()
                        got = up_in if upward else down_in
                        total[j, step] = (
                            parts[j, dest] + got[j, step - 1].astype(jnp.float32)
                        ).astype(jnp.bfloat16)

                hop(upward, j, step).start()

    def finish(j):
        where = pl.ds(j * CHUNK, CHUNK)
        out[:, where] = parts[j, place]

        @pl.when(has_down)
        def _():
            hop(True, j, LINES - 2).wait_recv()
            out[:, where] += up_in[j, LINES - 2].astype(jnp.float32)

        @pl.when(has_up)
        def _():
            hop(False, j, LINES - 2).wait_recv()
            out[:, where] += down_in[j, LINES - 2].astype(jnp.float32)

    for turn in range(chunks + 1):
        if turn < chunks:
            take(turn)
            send(turn, 0)
        if turn > 0:
            send(turn - 1, 2)
        if turn < chunks:
            send(turn, 1)
        if turn > 0:
            finish(turn - 1)
    for j in range(chunks):
        swap(j).wait_send()
        for step in range(LINES - 1):

            @pl.when(place <= step)
            def _(j=j, step=step):
                hop(True, j, step).wait_send()

            @pl.when(LINES - 1 - place <= step)
            def _(j=j, step=step):
                hop(False, j, step).wait_send()


def summed_product(columns, values, factor, ident):
    tiles = lax.axis_size("tile")
    (tokens, width), depth = columns.shape, values.shape[1]
    rows = width // tiles
    if tiles != 2 * LINES or rows % 16 or depth % CHUNK:
        whole = lax.dot_general(
            columns, values, (((0,), (0,)), ((), ())), preferred_element_type=jnp.float32
        )
        return lax.psum_scatter(whole * factor, "tile", scatter_dimension=0, tiled=True)
    chunks, hops = depth // CHUNK, LINES - 1
    line_buffer = pltpu.VMEM((chunks, hops, rows, CHUNK), jnp.bfloat16)
    pair_buffer = pltpu.VMEM((chunks, LINES, rows, CHUNK), jnp.bfloat16)
    return pl.pallas_call(
        functools.partial(sum_kernel, factor),
        out_shape=jax.ShapeDtypeStruct((rows, depth), jnp.float32),
        in_specs=[pl.BlockSpec(memory_space=pltpu.VMEM)] * 2,
        out_specs=pl.BlockSpec(memory_space=pltpu.VMEM),
        scratch_shapes=[
            pair_buffer,
            pair_buffer,
            pltpu.VMEM((chunks, LINES, rows, CHUNK), jnp.float32),
            *([line_buffer] * 4),
            *([pltpu.SemaphoreType.DMA((chunks,))] * 2),
            *([pltpu.SemaphoreType.DMA((chunks, hops))] * 4),
        ],
        compiler_params=pltpu.CompilerParams(
            collective_id=ident, has_side_effects=True, vmem_limit_bytes=36 * 1024 * 1024
        ),
        cost_estimate=pl.CostEstimate(
            flops=2 * tokens * width * depth,
            bytes_accessed=100_000_000,
            transcendentals=0,
        ),
    )(columns.T, values)


def shards(
    seq_grad, token_slot, pixels, dw_kernel, ln_gain, ln_bias, w_in, b_in, w_out, layer_scale
):
    tiles = lax.axis_size("tile")
    position = lax.axis_index("tile")
    band_index = (position + 1) % tiles
    slots = seq_grad.shape[0]
    capacity = slots // tiles
    tok_dev, chan_dev = pixels.shape
    reach = KSIZE // 2
    source = token_slot // slots
    local_slot = token_slot % slots
    onehot = (source[:, None] == jnp.arange(tiles, dtype=jnp.int32)[None, :]).astype(jnp.int32)
    ranks = jnp.sum((jnp.cumsum(onehot, axis=0) - onehot) * onehot, axis=1)
    seat = source * capacity + ranks
    seats = jnp.arange(tiles * capacity, dtype=jnp.int32)
    placed = seat[:, None] == seats[None, :]
    request = jnp.sum(jnp.where(placed, local_slot[:, None], 0), axis=0).reshape(tiles, capacity)
    asked = lax.all_to_all(request, "tile", split_axis=0, concat_axis=0, tiled=True)
    wanted = asked.reshape(-1, 1) == jnp.arange(slots, dtype=jnp.int32)[None, :]
    found = jnp.dot(
        wanted.astype(jnp.bfloat16), seq_grad, preferred_element_type=jnp.float32
    ).astype(jnp.bfloat16)
    arrived = lax.all_to_all(
        found.reshape(tiles, capacity, chan_dev), "tile", split_axis=0, concat_axis=0, tiled=True
    )
    rows = tok_dev // PAGE_SIDE
    tiles_page = PAGE_SIDE // rows
    grid = pixels.reshape(rows, PAGE_SIDE, chan_dev)
    extended = extended_2(grid, (("tile", 0),), reach)
    extended = after(extended, found)
    padded = page_edges(extended.astype(jnp.float32), band_index, tiles_page, reach)
    mixed = depthwise(padded, dw_kernel, rows, PAGE_SIDE).reshape(tok_dev, chan_dev)
    own_mean = jnp.mean(mixed, axis=1)
    own_center = mixed - own_mean[:, None]
    own_spread = jnp.sum(own_center * own_center, axis=1)
    own_stats = jnp.stack([own_mean, own_spread])
    chans = lax.axis_size("chan")
    stats = [own_stats] + [
        lax.ppermute(own_stats, "chan", [(i, (i + turn) % chans) for i in range(chans)])
        for turn in range(1, chans)
    ]
    mean = sum(one[0] for one in stats) / chans
    spread = sum(one[1] + chan_dev * (one[0] - mean) * (one[0] - mean) for one in stats)
    center = mixed - mean[:, None]
    inv_std = lax.rsqrt(spread / C + EPS)[:, None]
    normed = center * inv_std
    ln_part = (normed * ln_gain + ln_bias).astype(jnp.bfloat16)
    ln_out = lax.all_gather(ln_part, "chan", axis=1, tiled=True)
    arrived = after(arrived, ln_part)
    upstream = jnp.dot(
        placed.astype(jnp.bfloat16),
        arrived.reshape(tiles * capacity, chan_dev),
        preferred_element_type=jnp.float32,
    ).astype(jnp.bfloat16)
    upstream_all = lax.all_gather(upstream, "chan", axis=1, tiled=True)
    scaled = (upstream_all.astype(jnp.float32) * layer_scale).astype(jnp.bfloat16)
    preact = jnp.dot(ln_out, w_in, preferred_element_type=jnp.float32) + b_in
    act_val, act_slope = gelu_parts(preact)
    hidden = act_val.astype(jnp.bfloat16)
    factor = 1.0 / math.sqrt(tok_dev * tiles)
    back_hidden = lax.dot_general(
        scaled, w_out, (((1,), (1,)), ((), ())), preferred_element_type=jnp.float32
    )
    back_pre = (back_hidden * act_slope).astype(jnp.bfloat16)
    partial_sum = lax.dot_general(
        back_pre, w_in, (((1,), (1,)), ((), ())), preferred_element_type=jnp.float32
    ).astype(jnp.bfloat16)
    back_norm = lax.psum_scatter(partial_sum, "chan", scatter_dimension=1, tiled=True)
    grad_w_out = summed_product(scaled, after(hidden, partial_sum), factor, 0)
    back_norm = after(back_norm, grad_w_out).astype(jnp.float32)
    grad_normed = back_norm * ln_gain
    sum_grad, sum_cross = lax.psum(
        (jnp.sum(grad_normed, axis=1), jnp.sum(grad_normed * normed, axis=1)), "chan"
    )
    grad_mixed = inv_std * (
        grad_normed - (sum_grad / C)[:, None] - normed * (sum_cross / C)[:, None]
    )
    grad_grid = grad_mixed.reshape(rows, PAGE_SIDE, chan_dev)
    taps = []
    for row_off in range(KSIZE):
        for col_off in range(KSIZE):
            window = padded[row_off : row_off + rows, col_off : col_off + PAGE_SIDE, :]
            taps.append(jnp.sum(window * grad_grid, axis=(0, 1)))
    taps = jnp.stack(taps) * factor
    grad_kernel = lax.psum(taps, "tile")
    grad_ext = extended_2(grad_grid.astype(jnp.bfloat16), (("tile", 0),), reach)
    grad_w_in = summed_product(ln_out, after(back_pre, taps, grad_mixed), factor, 1)
    grad_pad = page_edges(
        after(grad_ext, grad_w_in).astype(jnp.float32), band_index, tiles_page, reach
    )
    back_conv = depthwise(grad_pad, dw_kernel[::-1], rows, PAGE_SIDE).reshape(tok_dev, chan_dev)
    grad_input = (upstream.astype(jnp.float32) + back_conv).astype(jnp.bfloat16)
    return (grad_input, grad_w_in, grad_w_out.T, grad_kernel)


def solution(mesh):
    placed = (
        P("tile", "chan"),
        P("tile"),
        P("tile", "chan"),
        P(None, "chan"),
        P("chan"),
        P("chan"),
        P(None, "chan"),
        P("chan"),
        P("chan", None),
        P(),
    )
    return jax.shard_map(
        shards,
        mesh=mesh,
        in_specs=placed,
        out_specs=(P("tile", "chan"), P("tile", "chan"), P("chan", "tile"), P(None, "chan")),
        check_vma=False,
    )
```

```python
import functools
import math

import jax
import jax.numpy as jnp
from jax import lax
from jax.experimental import pallas as pl
from jax.experimental.pallas import tpu as pltpu
from jax.sharding import PartitionSpec as P

C = 1536
KSIZE = 7
PAGE_SIDE = 48


EPS = 1e-06


def extended_2(value, sides, width):
    for axis, dim in sides:
        peers, length = (lax.axis_size(axis), value.shape[dim])
        up = [(i, (i + 1) % peers) for i in range(peers)]
        down = [(j, i) for i, j in up]
        last = lax.slice_in_dim(value, length - width, length, axis=dim)
        first = lax.slice_in_dim(value, 0, width, axis=dim)
        before = lax.ppermute(last, axis, up)
        after = lax.ppermute(first, axis, down)
        value = jnp.concatenate([before, value, after], axis=dim)
    return value


def gelu_parts(preact):
    normal_cdf = 0.5 * (1.0 + jax.scipy.special.erf(preact * 0.7071067811865476))
    density = jnp.exp(-0.5 * preact * preact) * 0.3989422804014327
    return (preact * normal_cdf, normal_cdf + preact * density)


def depthwise(padded, kernel, rows, cols):
    total = jnp.zeros((rows, cols, padded.shape[2]), jnp.float32)
    for row_off in range(KSIZE):
        for col_off in range(KSIZE):
            window = padded[row_off : row_off + rows, col_off : col_off + cols, :]
            total = total + kernel[row_off * KSIZE + col_off] * window
    return total


def page_edges(extended, band_index, tiles_page, reach):
    height = extended.shape[0]
    row_ids = lax.broadcasted_iota(jnp.int32, (height, 1, 1), 0)
    first = band_index % tiles_page == 0
    final = band_index % tiles_page == tiles_page - 1
    dropped = (row_ids < reach) & first | (row_ids >= height - reach) & final
    kept = jnp.where(dropped, jnp.zeros_like(extended), extended)
    return jnp.pad(kept, ((0, 0), (reach, reach), (0, 0)))


def after(value, *others):
    return lax.optimization_barrier((value, *others))[0]


LINES = 4
CHUNK = 256
MESH = pl.DeviceIdType.MESH


def sum_kernel(
    factor, columns, values, out, pair_out, pair_in, parts, up_out, up_in, down_out, down_in,
    lead_parts, lead_up_out, lead_up_in, lead_down_out, lead_down_in, pair_sent, pair_got, up_sent, up_got, down_sent, down_got,
):
    me = lax.axis_index("tile")
    side, place = me % 2, me // 2
    rows = columns.shape[0] // (2 * LINES)
    chunks = values.shape[1] // CHUNK
    pair = me + 1 - 2 * side
    has_up, has_down = place < LINES - 1, place > 0

    barrier = pltpu.get_barrier_semaphore()
    pl.semaphore_signal(barrier, inc=1, device_id={"tile": pair}, device_id_type=MESH)

    @pl.when(has_up)
    def _():
        pl.semaphore_signal(barrier, inc=1, device_id={"tile": me + 2}, device_id_type=MESH)

    @pl.when(has_down)
    def _():
        pl.semaphore_signal(barrier, inc=1, device_id={"tile": me - 2}, device_id_type=MESH)

    @pl.when(has_up & has_down)
    def _():
        pl.semaphore_wait(barrier, 3)

    @pl.when(jnp.logical_not(has_up & has_down))
    def _():
        pl.semaphore_wait(barrier, 2)

    def swap(j):
        return pltpu.make_async_remote_copy(
            src_ref=pair_out.at[j] if j else pair_out.at[0, 0],
            dst_ref=pair_in.at[j] if j else pair_in.at[0, 0],
            send_sem=pair_sent.at[j],
            recv_sem=pair_got.at[j],
            device_id={"tile": pair},
            device_id_type=MESH,
        )

    def buffers(upward, j):
        if j == 0:
            return (lead_up_out, lead_up_in) if upward else (lead_down_out, lead_down_in)
        out_ref, in_ref = (up_out, up_in) if upward else (down_out, down_in)
        return out_ref.at[j], in_ref.at[j]

    def hop(upward, j, step):
        src, dst = buffers(upward, j)
        sent, got = (up_sent, up_got) if upward else (down_sent, down_got)
        return pltpu.make_async_remote_copy(
            src_ref=src.at[step],
            dst_ref=dst.at[step],
            send_sem=sent.at[j, step],
            recv_sem=got.at[j, step],
            device_id={"tile": me + 2 if upward else me - 2},
            device_id_type=MESH,
        )

    def block(line, which, j):
        start = pl.multiple_of((2 * line + which) * rows, rows)
        return (
            jnp.dot(
                columns[pl.ds(start, rows), :],
                values[:, j * CHUNK : (j + 1) * CHUNK],
                preferred_element_type=jnp.float32,
            )
            * factor
        )

    def take(j):
        swap(j).wait_recv()
        parts[j] = parts[j] + pair_in[j].astype(jnp.float32)

    def send(j, step):
        for upward in (True, False):
            back = place if upward else LINES - 1 - place

            @pl.when(back <= step)
            def _(upward=upward, back=back):
                dest = LINES - 1 - step + place if upward else step - back
                total, got = buffers(upward, j)
                held = parts.at[j] if j else lead_parts
                total[step] = held[dest].astype(jnp.bfloat16)

                if step:

                    @pl.when(back > 0)
                    def _():
                        hop(upward, j, step - 1).wait_recv()
                        total[step] = (
                            held[dest] + got[step - 1].astype(jnp.float32)
                        ).astype(jnp.bfloat16)

                hop(upward, j, step).start()

    def finish(j):
        where = pl.ds(j * CHUNK, CHUNK)
        out[:, where] = parts[j, place]

        @pl.when(has_down)
        def _():
            hop(True, j, LINES - 2).wait_recv()
            out[:, where] += up_in[j, LINES - 2].astype(jnp.float32)

        @pl.when(has_up)
        def _():
            hop(False, j, LINES - 2).wait_recv()
            out[:, where] += down_in[j, LINES - 2].astype(jnp.float32)

    def offer(j):
        for line in range(LINES):
            pair_out[j, line] = block(line, 1 - side, j).astype(jnp.bfloat16)
        swap(j).start()

    offer(1)
    for line in range(LINES):
        for which in range(2):
            lead_parts[line, which * rows : (which + 1) * rows] = block(line, which, 0)
    send(0, 0)
    for j in range(2, chunks):
        offer(j)
    send(0, 1)
    for j in range(1, chunks):
        for line in range(LINES):
            parts[j, line] = block(line, side, j)
    send(0, 2)

    @pl.when(has_down)
    def _():
        hop(True, 0, LINES - 2).wait_recv()
        lead_parts[place] += lead_up_in[LINES - 2].astype(jnp.float32)

    @pl.when(has_up)
    def _():
        hop(False, 0, LINES - 2).wait_recv()
        lead_parts[place] += lead_down_in[LINES - 2].astype(jnp.float32)

    theirs = pl.ds(pl.multiple_of((1 - side) * rows, rows), rows)
    ours = pl.ds(pl.multiple_of(side * rows, rows), rows)
    pair_out[0, 0] = lead_parts[place, theirs].astype(jnp.bfloat16)
    swap(0).start()
    for turn in range(1, chunks + 1):
        if turn < chunks:
            take(turn)
            send(turn, 0)
        if turn > 1:
            send(turn - 1, 2)
        if turn < chunks:
            send(turn, 1)
        if turn > 1:
            finish(turn - 1)
    swap(0).wait_recv()
    out[:, 0:CHUNK] = lead_parts[place, ours] + pair_in[0, 0].astype(jnp.float32)
    for j in range(chunks):
        swap(j).wait_send()
        for step in range(LINES - 1):

            @pl.when(place <= step)
            def _(j=j, step=step):
                hop(True, j, step).wait_send()

            @pl.when(LINES - 1 - place <= step)
            def _(j=j, step=step):
                hop(False, j, step).wait_send()


def summed_product(columns, values, factor, ident):
    tiles = lax.axis_size("tile")
    (tokens, width), depth = columns.shape, values.shape[1]
    rows = width // tiles
    if tiles != 2 * LINES or rows % 16 or depth % CHUNK:
        whole = lax.dot_general(
            columns, values, (((0,), (0,)), ((), ())), preferred_element_type=jnp.float32
        )
        return lax.psum_scatter(whole * factor, "tile", scatter_dimension=0, tiled=True)
    chunks, hops = depth // CHUNK, LINES - 1
    line_buffer = pltpu.VMEM((chunks, hops, rows, CHUNK), jnp.bfloat16)
    pair_buffer = pltpu.VMEM((chunks, LINES, rows, CHUNK), jnp.bfloat16)
    return pl.pallas_call(
        functools.partial(sum_kernel, factor),
        out_shape=jax.ShapeDtypeStruct((rows, depth), jnp.float32),
        in_specs=[pl.BlockSpec(memory_space=pltpu.VMEM)] * 2,
        out_specs=pl.BlockSpec(memory_space=pltpu.VMEM),
        scratch_shapes=[
            pair_buffer,
            pair_buffer,
            pltpu.VMEM((chunks, LINES, rows, CHUNK), jnp.float32),
            *([line_buffer] * 4),
            pltpu.VMEM((LINES, 2 * rows, CHUNK), jnp.float32),
            *([pltpu.VMEM((hops, 2 * rows, CHUNK), jnp.bfloat16)] * 4),
            *([pltpu.SemaphoreType.DMA((chunks,))] * 2),
            *([pltpu.SemaphoreType.DMA((chunks, hops))] * 4),
        ],
        compiler_params=pltpu.CompilerParams(
            collective_id=ident, has_side_effects=True, vmem_limit_bytes=36 * 1024 * 1024
        ),
        cost_estimate=pl.CostEstimate(
            flops=2 * tokens * width * depth,
            bytes_accessed=100_000_000,
            transcendentals=0,
        ),
    )(columns.T, values)


def shards(
    seq_grad, token_slot, pixels, dw_kernel, ln_gain, ln_bias, w_in, b_in, w_out, layer_scale
):
    tiles = lax.axis_size("tile")
    position = lax.axis_index("tile")
    band_index = (position + 1) % tiles
    slots = seq_grad.shape[0]
    capacity = slots // tiles
    tok_dev, chan_dev = pixels.shape
    reach = KSIZE // 2
    source = token_slot // slots
    local_slot = token_slot % slots
    onehot = (source[:, None] == jnp.arange(tiles, dtype=jnp.int32)[None, :]).astype(jnp.int32)
    ranks = jnp.sum((jnp.cumsum(onehot, axis=0) - onehot) * onehot, axis=1)
    seat = source * capacity + ranks
    seats = jnp.arange(tiles * capacity, dtype=jnp.int32)
    placed = seat[:, None] == seats[None, :]
    request = jnp.sum(jnp.where(placed, local_slot[:, None], 0), axis=0).reshape(tiles, capacity)
    asked = lax.all_to_all(request, "tile", split_axis=0, concat_axis=0, tiled=True)
    wanted = asked.reshape(-1, 1) == jnp.arange(slots, dtype=jnp.int32)[None, :]
    found = jnp.dot(
        wanted.astype(jnp.bfloat16), seq_grad, preferred_element_type=jnp.float32
    ).astype(jnp.bfloat16)
    arrived = lax.all_to_all(
        found.reshape(tiles, capacity, chan_dev), "tile", split_axis=0, concat_axis=0, tiled=True
    )
    rows = tok_dev // PAGE_SIDE
    tiles_page = PAGE_SIDE // rows
    grid = pixels.reshape(rows, PAGE_SIDE, chan_dev)
    extended = extended_2(grid, (("tile", 0),), reach)
    extended = after(extended, found)
    padded = page_edges(extended.astype(jnp.float32), band_index, tiles_page, reach)
    mixed = depthwise(padded, dw_kernel, rows, PAGE_SIDE).reshape(tok_dev, chan_dev)
    own_mean = jnp.mean(mixed, axis=1)
    own_center = mixed - own_mean[:, None]
    own_spread = jnp.sum(own_center * own_center, axis=1)
    own_stats = jnp.stack([own_mean, own_spread])
    chans = lax.axis_size("chan")
    stats = [own_stats] + [
        lax.ppermute(own_stats, "chan", [(i, (i + turn) % chans) for i in range(chans)])
        for turn in range(1, chans)
    ]
    mean = sum(one[0] for one in stats) / chans
    spread = sum(one[1] + chan_dev * (one[0] - mean) * (one[0] - mean) for one in stats)
    center = mixed - mean[:, None]
    inv_std = lax.rsqrt(spread / C + EPS)[:, None]
    normed = center * inv_std
    ln_part = (normed * ln_gain + ln_bias).astype(jnp.bfloat16)
    ln_out = lax.all_gather(ln_part, "chan", axis=1, tiled=True)
    arrived = after(arrived, ln_part)
    upstream = jnp.dot(
        placed.astype(jnp.bfloat16),
        arrived.reshape(tiles * capacity, chan_dev),
        preferred_element_type=jnp.float32,
    ).astype(jnp.bfloat16)
    upstream_all = lax.all_gather(upstream, "chan", axis=1, tiled=True)
    scaled = (upstream_all.astype(jnp.float32) * layer_scale).astype(jnp.bfloat16)
    preact = jnp.dot(ln_out, w_in, preferred_element_type=jnp.float32) + b_in
    act_val, act_slope = gelu_parts(preact)
    hidden = act_val.astype(jnp.bfloat16)
    factor = 1.0 / math.sqrt(tok_dev * tiles)
    back_hidden = lax.dot_general(
        scaled, w_out, (((1,), (1,)), ((), ())), preferred_element_type=jnp.float32
    )
    back_pre = (back_hidden * act_slope).astype(jnp.bfloat16)
    partial_sum = lax.dot_general(
        back_pre, w_in, (((1,), (1,)), ((), ())), preferred_element_type=jnp.float32
    ).astype(jnp.bfloat16)
    back_norm = lax.psum_scatter(partial_sum, "chan", scatter_dimension=1, tiled=True)
    grad_w_out = summed_product(scaled, after(hidden, partial_sum), factor, 0)
    back_norm = after(back_norm, grad_w_out).astype(jnp.float32)
    grad_normed = back_norm * ln_gain
    sum_grad, sum_cross = lax.psum(
        (jnp.sum(grad_normed, axis=1), jnp.sum(grad_normed * normed, axis=1)), "chan"
    )
    grad_mixed = inv_std * (
        grad_normed - (sum_grad / C)[:, None] - normed * (sum_cross / C)[:, None]
    )
    grad_grid = grad_mixed.reshape(rows, PAGE_SIDE, chan_dev)
    taps = []
    for row_off in range(KSIZE):
        for col_off in range(KSIZE):
            window = padded[row_off : row_off + rows, col_off : col_off + PAGE_SIDE, :]
            taps.append(jnp.sum(window * grad_grid, axis=(0, 1)))
    taps = jnp.stack(taps) * factor
    grad_kernel = lax.psum(taps, "tile")
    grad_ext = extended_2(grad_grid.astype(jnp.bfloat16), (("tile", 0),), reach)
    grad_w_in = summed_product(ln_out, after(back_pre, taps, grad_mixed), factor, 1)
    grad_pad = page_edges(
        after(grad_ext, grad_w_in).astype(jnp.float32), band_index, tiles_page, reach
    )
    back_conv = depthwise(grad_pad, dw_kernel[::-1], rows, PAGE_SIDE).reshape(tok_dev, chan_dev)
    grad_input = (upstream.astype(jnp.float32) + back_conv).astype(jnp.bfloat16)
    return (grad_input, grad_w_in, grad_w_out.T, grad_kernel)


def solution(mesh):
    placed = (
        P("tile", "chan"),
        P("tile"),
        P("tile", "chan"),
        P(None, "chan"),
        P("chan"),
        P("chan"),
        P(None, "chan"),
        P("chan"),
        P("chan", None),
        P(),
    )
    return jax.shard_map(
        shards,
        mesh=mesh,
        in_specs=placed,
        out_specs=(P("tile", "chan"), P("tile", "chan"), P("chan", "tile"), P(None, "chan")),
        check_vma=False,
    )
```
